32 devices in a mesh: groups: 1, ep: 16 (over z, y, x), side: 2 (over core).
Axes of the slice: x: 2, y: 2, z: 4, core: 2. Of those that a mesh axis runs over, the one named last changes fastest.
Arguments:
- queries: bfloat16 [64, 36864], P(('groups', 'ep', 'side')), may hold values from -60 to 60
- latents: bfloat16 [64, 576, 512], P(('groups', 'ep', 'side')), may hold values from -4.5 to 4.5
- lengths: int32 [64], P(('groups', 'ep', 'side')), may hold values from 64 to 512, as said below
- tokens: bfloat16 [1024, 3584], P(('groups', 'ep', 'side')), may hold values from -30 to 30
- routes: int32 [1024, 8], P(('groups', 'ep', 'side')), may hold values from 0 to 15, all different within a row; in each aligned block of 32 rows (0 to 31, 32 to 63, ...) at most 32 rows name the same one
- router: bfloat16 [3584, 16], replicated, may hold values from -0.09375 to 0.09375
- gate_weight: bfloat16 [16, 3584, 1024], P('ep', None, 'side'), may hold values from -0.09375 to 0.09375
- up_weight: bfloat16 [16, 3584, 1024], P('ep', None, 'side'), may hold values from -0.09375 to 0.09375
- down_weight: bfloat16 [16, 1024, 3584], P('ep', 'side'), may hold values from -0.1875 to 0.1875
Outputs:
- attended: bfloat16 [64, 32768], P(('groups', 'ep', 'side'))
- moe: bfloat16 [1024, 3584], P(('groups', 'ep', 'side'))
The draws below stay inside these ranges and needn't reach their ends.
Inputs may be any that keep to these rules, and one draw needn't show every extreme that they name: `lengths`: some request of every draw has all 512 positions live. `routes`: among the rows of one device, no expert is named by more than 32 rows, a bound that some block reaches.
All inputs are finite; a program needn't handle non-finite values.
Results may differ from the reference program's by a relative error of at most 0.0072.
Values may be sent and summed in bfloat16 or wider, within the bound.
A program may use at most 128 MiB of HBM per device.

```python
import math
import jax
import jax.numpy as jnp
import numpy as np
from jax import lax

D = 3584
H = 1024
HEADS = 64
LATENT = 512
ROPE = 64
TOP = 8
LEN = 512
TOK_DEV = 32
EXPERTS = 16
CAP = 32
REQS = 64
TOKENS = 1024
N_EP = 16
N_SIDE = 2


def cache_base(key):
    return jnp.clip(jax.random.normal(jax.random.fold_in(key, 11), (REQS, LATENT + ROPE, LEN), jnp.float32), -4.5, 4.5)


def draw_latents(key, part):
    base = cache_base(key)
    return base.astype(jnp.bfloat16)


def draw_queries(key, part):
    key = jax.random.fold_in(key, 5)
    entries = jnp.clip(jax.random.normal(jax.random.fold_in(key, 1), (REQS, HEADS, LATENT + ROPE), jnp.float32), -4.5, 4.5)
    return entries.reshape(REQS, HEADS * (LATENT + ROPE)).astype(jnp.bfloat16)


def draw_tokens(key, part):
    key = jax.random.fold_in(key, 7)
    row_scale = jnp.exp(jax.random.uniform(jax.random.fold_in(key, 1), (TOKENS, 1), jnp.float32, -1.2, 1.1))
    column_scale = jnp.exp(jax.random.uniform(jax.random.fold_in(key, 2), (1, D), jnp.float32, -1.2, 1.1))
    noise = jax.random.normal(jax.random.fold_in(key, 3), (TOKENS, D), jnp.float32)
    return jnp.clip(noise * row_scale * column_scale, -30.0, 30.0).astype(jnp.bfloat16)


def draw_lengths(key, part):
    key = jax.random.fold_in(key, 9)
    drawn = jax.random.randint(jax.random.fold_in(key, 1), (REQS,), LEN // 8, LEN + 1, jnp.int32)
    longest = jax.random.randint(jax.random.fold_in(key, 2), (), 0, REQS, jnp.int32)
    return drawn.at[longest].set(LEN).astype(jnp.int32)


def level_of(own_key, shape, shards, least, largest):
    level = 1.0
    for position, shards_of in shards:
        steps = jax.random.uniform(jax.random.fold_in(jax.random.fold_in(own_key, 6), position), (shards_of,), jnp.float32, least / len(shards), largest / len(shards))
        level = level * jnp.repeat(jnp.exp(steps), shape[position] // shards_of).reshape((-1,) + (1,) * (len(shape) - 1 - position))
    return level


def routed_block(stream_key, own, number, rows, number_of, top, most, lean):
    sequence = jax.random.permutation(stream_key, number_of)
    packed, common = portions_of(number_of, rows * top, most, lean, True), portions_of(number_of, rows * top, most, lean, False)
    places = jnp.arange(number_of)

    def named(sizes, turn):
        used = int((sizes > 0).sum())
        fixed = max(1, used // 4)
        shifted = fixed + (places - fixed + turn * (used - fixed)) % max(1, number_of - fixed)
        return jnp.zeros((number_of,), jnp.int32).at[sequence[jnp.where(places < fixed, places, shifted)]].set(jnp.asarray(sizes, jnp.int32))

    sizes = jnp.where(number % 4 == 0, named(packed, number // 4), named(common, number - number // 4 - 1))
    mixed = jax.random.permutation(jax.random.fold_in(own, 3), number_of)
    donor, taker = mixed[0:number_of // 2 * 2:2], mixed[1:number_of // 2 * 2:2]
    margin = jnp.minimum(sizes[donor] - 1, most - sizes[taker]) // 2
    margin = jnp.where((donor == sequence[0]) | (taker == sequence[0]) | (sizes[taker] == 0), 0, jnp.maximum(margin, 0))
    shifted = jax.random.randint(jax.random.fold_in(own, 4), (number_of // 2,), 0, 1 << 20) % (margin + 1)
    sizes = sizes.at[donor].add(-shifted).at[taker].add(shifted)
    labels = jnp.searchsorted(jnp.cumsum(sizes), jnp.arange(rows * top), side="right").astype(jnp.int32)
    listing = labels.reshape(top, rows).T
    listing = listing[jax.random.permutation(jax.random.fold_in(own, 1), rows)]
    turn = jax.random.randint(jax.random.fold_in(own, 2), (rows, 1), 0, top)
    return jnp.take_along_axis(listing, (jnp.arange(top)[None, :] + turn) % top, axis=1)


def portions_of(count, total, most, skew, full):
    weights = [(1 << 20) // math.isqrt(rank ** skew) + 1 for rank in range(1, count + 1)]
    largest = most if full else min(most, max(-(-total // count), total * weights[0] // sum(weights)))
    least = 1 if total - largest >= count - 1 else 0
    holding, spare = [largest] + [least] * (count - 1), total - largest - least * (count - 1)
    while spare > 0:
        free = [i for i in range(1, count) if holding[i] < largest] or [i for i in range(1, count) if holding[i] < most]
        pool, remaining = sum([weights[i] for i in free]), spare
        for i in free:
            more = min(most - holding[i], max(1, remaining * weights[i] // pool), spare)
            holding[i] = holding[i] + more
            spare = spare - more
    return np.array(holding)


def scatter_about(own_key, dims, spread, limit, split=(), kind=jnp.bfloat16):
    values = jax.random.normal(own_key, dims, jnp.float32) * spread
    if len(split) > 0:
        values = level_of(own_key, dims, split, -0.22, 0.18) * values
    return jnp.clip(values, min=-limit, max=limit).astype(kind)


def setup_inputs(seed: int = 0, part: int = 0) -> dict:
    key_of = jax.random.split(jax.random.key(seed), 10)
    part_splits = jax.random.split(jax.random.fold_in(key_of[9], part), 10)
    queries = draw_queries(jax.random.fold_in(jax.random.fold_in(key_of[9], part), 71), part)
    latents = draw_latents(jax.random.fold_in(jax.random.fold_in(key_of[9], part), 71), part)
    lengths = draw_lengths(jax.random.fold_in(jax.random.fold_in(key_of[9], part), 71), part)
    tokens = draw_tokens(jax.random.fold_in(jax.random.fold_in(key_of[9], part), 71), part)
    routes_keys = jax.random.split(jax.random.fold_in(part_splits[4], 1), TOKENS // TOK_DEV)
    routes_turns = jax.random.permutation(jax.random.fold_in(part_splits[4], 3), TOKENS // TOK_DEV)
    routes = jax.vmap(lambda own, number: routed_block(jax.random.fold_in(part_splits[4], 2), own, number, TOK_DEV, EXPERTS, TOP, CAP, 2))(routes_keys, routes_turns).reshape((TOKENS, TOP))
    router = scatter_about(key_of[5], (D, EXPERTS), D ** -0.5, 0.09375)
    gate_weight = scatter_about(key_of[6], (EXPERTS, D, H), D ** -0.5, 0.09375, ((0, 16), (2, 2)))
    up_weight = scatter_about(key_of[7], (EXPERTS, D, H), D ** -0.5, 0.09375, ((0, 16), (2, 2)))
    down_weight = scatter_about(key_of[8], (EXPERTS, H, D), H ** -0.5, 0.1875, ((0, 16), (1, 2)))
    return dict(queries=queries, latents=latents, lengths=lengths, tokens=tokens, routes=routes, router=router, gate_weight=gate_weight, up_weight=up_weight, down_weight=down_weight)


SOFT_SCALE = 192.0 ** (-0.5)
ROUTE_SCALE = 2.5
NORM_EPS = 1e-06

def attend_request(query_row, cache_block, length):
    head_queries = query_row.reshape(HEADS, LATENT + ROPE)
    scores = jnp.dot(head_queries, cache_block, preferred_element_type=jnp.float32) * SOFT_SCALE
    live = lax.broadcasted_iota(jnp.int32, (1, LEN), 1) < length
    scores = jnp.where(live, scores, -1e+30)
    highest = lax.optimization_barrier(jnp.max(scores, axis=1, keepdims=True))
    powers = jnp.where(live, jnp.exp(scores - highest), 0.0)
    probs = (powers / lax.optimization_barrier(jnp.sum(powers, axis=1, keepdims=True))).astype(jnp.bfloat16)
    mixed = lax.dot_general(probs, cache_block[:LATENT], (((1,), (1,)), ((), ())), preferred_element_type=jnp.float32)
    return mixed.astype(jnp.bfloat16).reshape(HEADS * LATENT)

def expert_block(rows, gate_matrix, up_matrix, down_matrix):
    gate = jnp.dot(rows, gate_matrix, preferred_element_type=jnp.float32)
    up = jnp.dot(rows, up_matrix, preferred_element_type=jnp.float32)
    hidden = (jax.nn.silu(gate) * up).astype(jnp.bfloat16)
    return jnp.dot(hidden, down_matrix, preferred_element_type=jnp.float32)

def normalize(tokens):
    values = tokens.astype(jnp.float32)
    mean_square = lax.optimization_barrier(jnp.mean(values * values, axis=1, keepdims=True))
    return (values * lax.rsqrt(mean_square + NORM_EPS)).astype(jnp.bfloat16)

def reference(queries, latents, lengths, tokens, routes, router, gate_weight, up_weight, down_weight):
    attended = lax.map(lambda item: attend_request(item[0], item[1], item[2]), (queries, latents, lengths))
    normed = normalize(tokens)
    affinity = jax.nn.sigmoid(jnp.dot(normed, router, preferred_element_type=jnp.float32))
    chosen = jnp.take_along_axis(affinity, routes, axis=1)
    gates = chosen / lax.optimization_barrier(jnp.sum(chosen, axis=1, keepdims=True)) * ROUTE_SCALE
    flat = routes.reshape(-1).astype(jnp.int32)
    order = jnp.argsort(flat, stable=True).astype(jnp.int32)
    counts = lax.optimization_barrier(jnp.sum((flat[None, :] == jnp.arange(EXPERTS, dtype=jnp.int32)[:, None]).astype(jnp.int32), axis=1)).astype(jnp.int32)
    starts = (jnp.cumsum(counts) - counts).astype(jnp.int32)
    most_rows = N_EP * N_SIDE * CAP
    owners = jnp.concatenate([(order // TOP).astype(jnp.int32), jnp.zeros((most_rows,), jnp.int32)]).astype(jnp.int32)
    shares = jnp.concatenate([gates.reshape(-1)[order], jnp.zeros((most_rows,), jnp.float32)])

    def one_expert(carried, index):
        start = starts[index]
        owner_rows = lax.dynamic_slice_in_dim(owners, start, most_rows, 0)
        share = lax.dynamic_slice_in_dim(shares, start, most_rows, 0)
        live = jnp.arange(most_rows, dtype=jnp.int32) < counts[index]
        share = jnp.where(live, share, 0.0)
        expert_out = expert_block(normed[owner_rows], gate_weight[index], up_weight[index], down_weight[index]).astype(jnp.bfloat16)
        carried = carried.at[owner_rows].add(expert_out.astype(jnp.float32) * share[:, None])
        return (carried, None)
    total, unused = lax.scan(one_expert, jnp.zeros((TOKENS, D), jnp.float32), jnp.arange(EXPERTS, dtype=jnp.int32))
    return (attended, total.astype(jnp.bfloat16))
```

```python
import jax
import jax.numpy as jnp
from jax import lax
from jax.sharding import PartitionSpec as P

LATENT = 512


SOFT_SCALE = 192.0 ** (-0.5)
ROUTE_SCALE = 2.5
NORM_EPS = 1e-06


def attend_request(query_row, cache_block, length):
    positions = cache_block.shape[1]
    head_queries = query_row.reshape(-1, cache_block.shape[0])
    scores = jnp.dot(head_queries, cache_block, preferred_element_type=jnp.float32) * SOFT_SCALE
    live = lax.broadcasted_iota(jnp.int32, (1, positions), 1) < length
    scores = jnp.where(live, scores, -1e30)
    highest = jnp.max(scores, axis=1, keepdims=True)
    powers = jnp.where(live, jnp.exp(scores - highest), 0.0)
    probs = (powers / jnp.sum(powers, axis=1, keepdims=True)).astype(jnp.bfloat16)
    mixed = lax.dot_general(
        probs, cache_block[:LATENT], (((1,), (1,)), ((), ())), preferred_element_type=jnp.float32
    )
    return mixed.astype(jnp.bfloat16).reshape(-1)


def expert_block(rows, gate_matrix, up_matrix, down_matrix):
    gate = jnp.dot(rows, gate_matrix, preferred_element_type=jnp.float32)
    up = jnp.dot(rows, up_matrix, preferred_element_type=jnp.float32)
    hidden = (jax.nn.silu(gate) * up).astype(jnp.bfloat16)
    return jnp.dot(hidden, down_matrix, preferred_element_type=jnp.float32)


def expert_rows(rows, valid, gate_matrix, up_matrix, down_matrix):
    return jnp.where(valid[:, None], expert_block(rows, gate_matrix, up_matrix, down_matrix), 0.0)


def slot_mask(counts, capacity):
    return (
        lax.broadcasted_iota(jnp.int32, (counts.shape[0], capacity), 1) < counts[:, None]
    ).reshape(-1)


def body(queries, latents, lengths, tokens, routes, router, gate_weight, up_weight, down_weight):
    attended = jax.vmap(attend_request)(queries, latents, lengths)
    experts = lax.axis_size("ep")
    token_count, top_count = routes.shape
    width = tokens.shape[1]
    capacity = min(token_count, 2 * token_count * top_count // experts)
    values = tokens.astype(jnp.float32)
    mean_square = jnp.mean(values * values, axis=1, keepdims=True)
    normed = (values * lax.rsqrt(mean_square + NORM_EPS)).astype(jnp.bfloat16)
    affinity = jax.nn.sigmoid(jnp.dot(normed, router, preferred_element_type=jnp.float32))
    one_hot = routes[:, :, None] == lax.broadcasted_iota(jnp.int32, (1, 1, experts), 2)
    chosen = jnp.sum(jnp.where(one_hot, affinity[:, None, :], 0.0), axis=2)
    gates = chosen / jnp.sum(chosen, axis=1, keepdims=True) * ROUTE_SCALE
    if capacity == token_count:
        both = ("ep", "side")
        dense = jnp.sum(jnp.where(one_hot, gates[:, :, None], 0.0), axis=1)
        rows = lax.all_gather(normed, both, axis=0, tiled=True)
        shares = lax.all_gather(dense, both, axis=0, tiled=True)
        share = lax.dynamic_slice_in_dim(shares, lax.axis_index("ep"), 1, 1)
        gate = jnp.dot(rows, gate_weight[0], preferred_element_type=jnp.float32)
        up = jnp.dot(rows, up_weight[0], preferred_element_type=jnp.float32)
        hidden = (jax.nn.silu(gate) * up * share).astype(jnp.bfloat16)
        partial = jnp.dot(hidden, down_weight[0], preferred_element_type=jnp.float32)
        moe = lax.psum_scatter(
            partial.astype(jnp.bfloat16), both, scatter_dimension=0, tiled=True
        )
        return (attended, moe)
    flat_hot = one_hot.reshape(-1, experts).astype(jnp.int32)
    slot = jnp.sum((jnp.cumsum(flat_hot, axis=0) - flat_hot) * flat_hot, axis=1)
    counts = jnp.sum(flat_hot, axis=0)
    target = routes.reshape(-1) * capacity + slot
    outgoing = (
        jnp.zeros((experts * capacity, width), jnp.bfloat16)
        .at[target]
        .set(jnp.repeat(normed, top_count, axis=0))
    )
    outgoing = outgoing.reshape(experts, capacity, width)
    gate_matrix = gate_weight[0]
    up_matrix = up_weight[0]
    down_matrix = down_weight[0]
    arrived, arrived_counts = (
        lax.all_to_all(outgoing, "ep", split_axis=0, concat_axis=0, tiled=True),
        lax.all_to_all(counts, "ep", split_axis=0, concat_axis=0, tiled=True),
    )
    paired, paired_counts = (
        lax.all_gather(arrived, "side", axis=0, tiled=True),
        lax.all_gather(arrived_counts, "side", axis=0, tiled=True),
    )
    paired_rows = paired.reshape(-1, width)
    valid = slot_mask(paired_counts, capacity)
    summed = lax.psum_scatter(
        expert_rows(paired_rows, valid, gate_matrix, up_matrix, down_matrix),
        "side",
        scatter_dimension=0,
        tiled=True,
    )
    returned = lax.all_to_all(
        summed.astype(jnp.bfloat16).reshape(experts, capacity, width),
        "ep",
        split_axis=0,
        concat_axis=0,
        tiled=True,
    )
    picked = returned.reshape(experts * capacity, width)[target]
    weighted = picked.reshape(token_count, top_count, width).astype(jnp.float32) * gates[:, :, None]
    moe = jnp.sum(weighted, axis=1)
    return (attended, moe.astype(jnp.bfloat16))


def solution(mesh):
    return jax.shard_map(
        body,
        mesh=mesh,
        in_specs=(
            P(("groups", "ep", "side"), None),
            P(("groups", "ep", "side"), None, None),
            P(("groups", "ep", "side")),
            P(("groups", "ep", "side"), None),
            P(("groups", "ep", "side"), None),
            P(),
            P("ep", None, "side"),
            P("ep", None, "side"),
            P("ep", "side", None),
        ),
        out_specs=(P(("groups", "ep", "side"), None), P(("groups", "ep", "side"), None)),
        check_vma=False,
    )
```

```python
import functools

import jax
import jax.numpy as jnp
from jax import lax
from jax.experimental import pallas as pl
from jax.experimental.pallas import tpu as pltpu
from jax.sharding import PartitionSpec as P

LATENT = 512


SOFT_SCALE = 192.0 ** (-0.5)
ROUTE_SCALE = 2.5
NORM_EPS = 1e-06


def attend_request(query_row, cache_block, length):
    positions = cache_block.shape[1]
    head_queries = query_row.reshape(-1, cache_block.shape[0])
    scores = jnp.dot(head_queries, cache_block, preferred_element_type=jnp.float32) * SOFT_SCALE
    live = lax.broadcasted_iota(jnp.int32, (1, positions), 1) < length
    scores = jnp.where(live, scores, -1e30)
    highest = jnp.max(scores, axis=1, keepdims=True)
    powers = jnp.where(live, jnp.exp(scores - highest), 0.0)
    probs = (powers / jnp.sum(powers, axis=1, keepdims=True)).astype(jnp.bfloat16)
    mixed = lax.dot_general(
        probs, cache_block[:LATENT], (((1,), (1,)), ((), ())), preferred_element_type=jnp.float32
    )
    return mixed.astype(jnp.bfloat16).reshape(-1)


def expert_block(rows, gate_matrix, up_matrix, down_matrix):
    gate = jnp.dot(rows, gate_matrix, preferred_element_type=jnp.float32)
    up = jnp.dot(rows, up_matrix, preferred_element_type=jnp.float32)
    hidden = (jax.nn.silu(gate) * up).astype(jnp.bfloat16)
    return jnp.dot(hidden, down_matrix, preferred_element_type=jnp.float32)


def expert_rows(rows, valid, gate_matrix, up_matrix, down_matrix):
    return jnp.where(valid[:, None], expert_block(rows, gate_matrix, up_matrix, down_matrix), 0.0)


def slot_mask(counts, capacity):
    return (
        lax.broadcasted_iota(jnp.int32, (counts.shape[0], capacity), 1) < counts[:, None]
    ).reshape(-1)


PLANE = 4
GATE_LANES = 128
LOW_LANE = 64
COPIES = 112


def dense_kernel(
    depth, a0, a1, wg_hbm, wu_hbm, wd_hbm, out,
    x0, x1, wg, wu, wd, hid, acc, so, sr, b1, r1, b2, r2, b3, r3, wsem, ssem, rsem,
):
    rows = a0.shape[0]
    half = a1.shape[1]
    me = lax.axis_index("ep")
    side = lax.axis_index("side")
    plane = me // PLANE
    g0 = me % PLANE
    x, y = g0 % 2, g0 // 2
    gx = y * 2 + (1 - x)
    gy = (1 - y) * 2 + x
    gd = (1 - y) * 2 + (1 - x)
    base = plane * PLANE
    to_x, to_y = {"ep": base + gx}, {"ep": base + gy}
    to_side = {"side": 1 - side}
    to_plane = [None] + [{"ep": (plane + d) % depth * PLANE + g0} for d in range(1, depth)]
    first, second = (to_x, to_y), (to_y, to_x)
    near, far = (gx, gy), (gy, gx)
    mesh_ids = pl.DeviceIdType.MESH
    started = []

    def send(src, dst, target):
        k = len(started)
        copy = pltpu.make_async_remote_copy(
            src_ref=src, dst_ref=dst, send_sem=ssem.at[k], recv_sem=rsem.at[k],
            device_id=target, device_id_type=mesh_ids,
        )
        copy.start()
        started.append(copy)
        return copy

    loads = [
        pltpu.make_async_copy(wg_hbm, wg, wsem.at[0]),
        pltpu.make_async_copy(wu_hbm, wu, wsem.at[1]),
        pltpu.make_async_copy(wd_hbm, wd, wsem.at[2]),
    ]
    for load in loads:
        load.start()

    barrier = pltpu.get_barrier_semaphore()
    partners = [to_x, to_y, to_side] + to_plane[1:]
    for target in partners:
        pl.semaphore_signal(barrier, inc=1, device_id=target, device_id_type=mesh_ids)
    pl.semaphore_wait(barrier, len(partners))

    own = (a0, a1)
    full = (x0, x1)
    order = list(range(1, depth)) + [0]

    def span(d):
        return pl.ds(pl.multiple_of((plane + d) % depth * rows, rows), rows)

    def slot(h, g, d):
        return full[h].at[g, side, span(-d + depth)]

    by_plane = {}
    for d in range(1, depth):
        for h in range(2):
            by_plane[h, d] = send(own[h], slot(h, g0, 0), to_plane[d])
    by_first, by_second, by_far, by_side = {}, {}, {}, {}

    def spread(h, d):
        block = own[h] if d == 0 else slot(h, g0, d)
        by_first[h, d] = send(block, slot(h, g0, d), first[h])
        by_second[h, d] = send(block, slot(h, g0, d), second[h])
        by_side[h, 0, d] = send(block, slot(h, g0, d), to_side)

    def pass_on(h, d):
        by_first[h, d].wait_recv()
        block = slot(h, near[h], d)
        by_far[h, d] = send(block, block, second[h])
        by_side[h, 1, d] = send(block, block, to_side)

    for h in range(2):
        spread(h, 0)
        full[h][g0, side, span(0)] = own[h][...]
    for d in range(1, depth):
        for h in range(2):
            by_plane[h, d].wait_recv()
            spread(h, d)
        for h in range(2):
            pass_on(h, d - 1)
    for h in range(2):
        pass_on(h, depth - 1)
    for d in range(depth):
        for h in range(2):
            by_second[h, d].wait_recv()
            block = slot(h, far[h], d)
            by_side[h, 2, d] = send(block, block, to_side)

    lanes = lax.broadcasted_iota(jnp.int32, (1, GATE_LANES), 1)
    mine = (lanes == me) | (lanes == me + LOW_LANE)

    def both_sides(ref, g, columns):
        return jnp.concatenate([ref[g, side, :, columns], ref[g, 1 - side, :, columns]], axis=0)

    group_rows = x0.shape[2]
    wide = 256
    deep = 512

    def compute(g):
        tail = both_sides(x0, g, pl.ds(half, GATE_LANES)).astype(jnp.float32)
        share = jnp.sum(jnp.where(mine, tail, 0.0), axis=1, keepdims=True)

        @pl.loop(0, wg.shape[1] // wide)
        def _(n):
            columns = pl.ds(pl.multiple_of(n * wide, wide), wide)
            rows0 = both_sides(x0, g, pl.ds(0, half))
            rows1 = both_sides(x1, g, pl.ds(0, half))
            gate = jnp.dot(rows0, wg[pl.ds(0, half), columns], preferred_element_type=jnp.float32)
            gate += jnp.dot(rows1, wg[pl.ds(half, half), columns], preferred_element_type=jnp.float32)
            up = jnp.dot(rows0, wu[pl.ds(0, half), columns], preferred_element_type=jnp.float32)
            up += jnp.dot(rows1, wu[pl.ds(half, half), columns], preferred_element_type=jnp.float32)
            hidden = gate / (1.0 + jnp.exp(-gate)) * up * share
            hid[:, columns] = hidden.astype(jnp.bfloat16)

        @pl.loop(0, wd.shape[1] // deep)
        def _(n):
            columns = pl.ds(pl.multiple_of(n * deep, deep), deep)
            result = jnp.dot(hid[...], wd[:, columns], preferred_element_type=jnp.float32)
            acc[g, :, columns] = result[:group_rows]
            so[g, :, columns] = result[group_rows:].astype(jnp.bfloat16)

        return send(so.at[g], sr.at[g], to_side)

    def features(h):
        return pl.ds(h * half, half)

    def chip_sum(g, h, d):
        part = sr[g, span(d), features(h)].astype(jnp.float32)
        return acc[g, span(d), features(h)] + part

    def f32(ref, *index):
        return ref[index].astype(jnp.float32)

    back1, back2, back3 = {}, {}, {}

    def to_second(g, h, i, d):
        b1[h, i, d] = chip_sum(g, h, d).astype(jnp.bfloat16)
        back1[h, i, d] = send(b1.at[h, i, d], r1.at[h, i, d], second[h])

    def arrived(j, halves):
        for d in range(depth):
            for h in halves:
                by_side[h, j, d].wait_recv()

    for load in loads:
        load.wait()
    arrived(0, (0, 1))
    side0 = compute(g0)
    arrived(1, (0,))
    arrived(2, (1,))
    sidex = compute(gx)
    arrived(1, (1,))
    arrived(2, (0,))
    for d in range(depth):
        for h in range(2):
            by_far[h, d].wait_recv()
            block = slot(h, gd, d)
            by_side[h, 3, d] = send(block, block, to_side)
    sidex.wait_recv()
    for d in order:
        to_second(gx, 1, 0, d)
    sidey = compute(gy)
    arrived(3, (0, 1))
    sidey.wait_recv()
    for d in order:
        to_second(gy, 0, 0, d)
    sided = compute(gd)
    side0.wait_recv()
    sided.wait_recv()
    for d in order:
        for h in range(2):
            to_second(gd, h, 1, d)

    def to_first(h, d):
        back1[h, 1, d].wait_recv()
        total = chip_sum(near[h], h, d) + f32(r1, h, 1, d)
        b2[h, d] = total.astype(jnp.bfloat16)
        back2[h, d] = send(b2.at[h, d], r2.at[h, d], first[h])

    def plane_sum(h, d):
        back1[h, 0, d].wait_recv()
        back2[h, d].wait_recv()
        return chip_sum(g0, h, d) + f32(r1, h, 0, d) + f32(r2, h, d)

    def to_owner(h, d):
        b3[h, d - 1] = plane_sum(h, d).astype(jnp.bfloat16)
        back3[h, d] = send(b3.at[h, d - 1], r3.at[h, d - 1], to_plane[d])

    for i, d in enumerate(order):
        for h in range(2):
            to_first(h, d)
        if i > 0:
            for h in range(2):
                to_owner(h, order[i - 1])
    for h in range(2):
        total = plane_sum(h, 0)
        for d in range(1, depth):
            back3[h, d].wait_recv()
            total += f32(r3, h, d - 1)
        out[:, features(h)] = total.astype(jnp.bfloat16)
    for copy in started:
        copy.wait_send()


def dense_moe(normed, dense, gate_matrix, up_matrix, down_matrix):
    count, width = normed.shape
    devices, experts = lax.axis_size("ep"), dense.shape[1]
    half = width // 2
    depth = devices // PLANE
    high = dense.astype(jnp.bfloat16)
    low = (dense - high.astype(jnp.float32)).astype(jnp.bfloat16)
    pad = jnp.zeros((count, LOW_LANE - experts), jnp.bfloat16)
    a0 = jnp.concatenate([normed[:, :half], high, pad, low, pad], axis=1)
    a1 = normed[:, half:]
    rows = depth * count
    bf16 = jnp.bfloat16
    vmem = pl.BlockSpec(memory_space=pltpu.VMEM)
    hbm = pl.BlockSpec(memory_space=pl.ANY)
    hidden_units = gate_matrix.shape[1]
    return pl.pallas_call(
        functools.partial(dense_kernel, depth),
        out_shape=jax.ShapeDtypeStruct((count, width), bf16),
        in_specs=[vmem, vmem, hbm, hbm, hbm],
        out_specs=vmem,
        scratch_shapes=[
            pltpu.VMEM((PLANE, 2, rows, half + GATE_LANES), bf16),
            pltpu.VMEM((PLANE, 2, rows, half), bf16),
            pltpu.VMEM(gate_matrix.shape, bf16),
            pltpu.VMEM(up_matrix.shape, bf16),
            pltpu.VMEM(down_matrix.shape, bf16),
            pltpu.VMEM((2 * rows, hidden_units), bf16),
            pltpu.VMEM((PLANE, rows, width), jnp.float32),
            pltpu.VMEM((PLANE, rows, width), bf16),
            pltpu.VMEM((PLANE, rows, width), bf16),
            pltpu.VMEM((2, 2, depth, count, half), bf16),
            pltpu.VMEM((2, 2, depth, count, half), bf16),
            pltpu.VMEM((2, depth, count, half), bf16),
            pltpu.VMEM((2, depth, count, half), bf16),
            pltpu.VMEM((2, depth - 1, count, half), bf16),
            pltpu.VMEM((2, depth - 1, count, half), bf16),
            pltpu.SemaphoreType.DMA((3,)),
            pltpu.SemaphoreType.DMA((COPIES,)),
            pltpu.SemaphoreType.DMA((COPIES,)),
        ],
        compiler_params=pltpu.CompilerParams(
            collective_id=0, has_side_effects=True, vmem_limit_bytes=56 * 1024 * 1024
        ),
        cost_estimate=pl.CostEstimate(
            flops=12 * PLANE * rows * width * hidden_units,
            bytes_accessed=6 * width * hidden_units,
            transcendentals=0,
        ),
    )(a0, a1, gate_matrix, up_matrix, down_matrix)


def body(queries, latents, lengths, tokens, routes, router, gate_weight, up_weight, down_weight):
    attended = jax.vmap(attend_request)(queries, latents, lengths)
    experts = lax.axis_size("ep")
    token_count, top_count = routes.shape
    width = tokens.shape[1]
    capacity = min(token_count, 2 * token_count * top_count // experts)
    values = tokens.astype(jnp.float32)
    mean_square = jnp.mean(values * values, axis=1, keepdims=True)
    normed = (values * lax.rsqrt(mean_square + NORM_EPS)).astype(jnp.bfloat16)
    affinity = jax.nn.sigmoid(jnp.dot(normed, router, preferred_element_type=jnp.float32))
    one_hot = routes[:, :, None] == lax.broadcasted_iota(jnp.int32, (1, 1, experts), 2)
    chosen = jnp.sum(jnp.where(one_hot, affinity[:, None, :], 0.0), axis=2)
    gates = chosen / jnp.sum(chosen, axis=1, keepdims=True) * ROUTE_SCALE
    if capacity == token_count and experts % PLANE == 0 and experts <= LOW_LANE:
        dense = jnp.sum(jnp.where(one_hot, gates[:, :, None], 0.0), axis=1)
        moe = dense_moe(normed, dense, gate_weight[0], up_weight[0], down_weight[0])
        return (attended, moe)
    flat_hot = one_hot.reshape(-1, experts).astype(jnp.int32)
    slot = jnp.sum((jnp.cumsum(flat_hot, axis=0) - flat_hot) * flat_hot, axis=1)
    counts = jnp.sum(flat_hot, axis=0)
    target = routes.reshape(-1) * capacity + slot
    outgoing = (
        jnp.zeros((experts * capacity, width), jnp.bfloat16)
        .at[target]
        .set(jnp.repeat(normed, top_count, axis=0))
    )
    outgoing = outgoing.reshape(experts, capacity, width)
    gate_matrix = gate_weight[0]
    up_matrix = up_weight[0]
    down_matrix = down_weight[0]
    arrived, arrived_counts = (
        lax.all_to_all(outgoing, "ep", split_axis=0, concat_axis=0, tiled=True),
        lax.all_to_all(counts, "ep", split_axis=0, concat_axis=0, tiled=True),
    )
    paired, paired_counts = (
        lax.all_gather(arrived, "side", axis=0, tiled=True),
        lax.all_gather(arrived_counts, "side", axis=0, tiled=True),
    )
    paired_rows = paired.reshape(-1, width)
    valid = slot_mask(paired_counts, capacity)
    summed = lax.psum_scatter(
        expert_rows(paired_rows, valid, gate_matrix, up_matrix, down_matrix),
        "side",
        scatter_dimension=0,
        tiled=True,
    )
    returned = lax.all_to_all(
        summed.astype(jnp.bfloat16).reshape(experts, capacity, width),
        "ep",
        split_axis=0,
        concat_axis=0,
        tiled=True,
    )
    picked = returned.reshape(experts * capacity, width)[target]
    weighted = picked.reshape(token_count, top_count, width).astype(jnp.float32) * gates[:, :, None]
    moe = jnp.sum(weighted, axis=1)
    return (attended, moe.astype(jnp.bfloat16))


def solution(mesh):
    return jax.shard_map(
        body,
        mesh=mesh,
        in_specs=(
            P(("groups", "ep", "side"), None),
            P(("groups", "ep", "side"), None, None),
            P(("groups", "ep", "side")),
            P(("groups", "ep", "side"), None),
            P(("groups", "ep", "side"), None),
            P(),
            P("ep", None, "side"),
            P("ep", None, "side"),
            P("ep", "side", None),
        ),
        out_specs=(P(("groups", "ep", "side"), None), P(("groups", "ep", "side"), None)),
        check_vma=False,
    )
```

```python
import functools

import jax
import jax.numpy as jnp
from jax import lax
from jax.experimental import pallas as pl
from jax.experimental.pallas import tpu as pltpu
from jax.sharding import PartitionSpec as P

LATENT = 512


SOFT_SCALE = 192.0 ** (-0.5)
ROUTE_SCALE = 2.5
NORM_EPS = 1e-06


def attend_request(query_row, cache_block, length):
    positions = cache_block.shape[1]
    head_queries = query_row.reshape(-1, cache_block.shape[0])
    scores = jnp.dot(head_queries, cache_block, preferred_element_type=jnp.float32) * SOFT_SCALE
    live = lax.broadcasted_iota(jnp.int32, (1, positions), 1) < length
    scores = jnp.where(live, scores, -1e30)
    highest = jnp.max(scores, axis=1, keepdims=True)
    powers = jnp.where(live, jnp.exp(scores - highest), 0.0)
    probs = (powers / jnp.sum(powers, axis=1, keepdims=True)).astype(jnp.bfloat16)
    mixed = lax.dot_general(
        probs, cache_block[:LATENT], (((1,), (1,)), ((), ())), preferred_element_type=jnp.float32
    )
    return mixed.astype(jnp.bfloat16).reshape(-1)


def expert_block(rows, gate_matrix, up_matrix, down_matrix):
    gate = jnp.dot(rows, gate_matrix, preferred_element_type=jnp.float32)
    up = jnp.dot(rows, up_matrix, preferred_element_type=jnp.float32)
    hidden = (jax.nn.silu(gate) * up).astype(jnp.bfloat16)
    return jnp.dot(hidden, down_matrix, preferred_element_type=jnp.float32)


def expert_rows(rows, valid, gate_matrix, up_matrix, down_matrix):
    return jnp.where(valid[:, None], expert_block(rows, gate_matrix, up_matrix, down_matrix), 0.0)


def slot_mask(counts, capacity):
    return (
        lax.broadcasted_iota(jnp.int32, (counts.shape[0], capacity), 1) < counts[:, None]
    ).reshape(-1)


PLANE = 4
GATE_LANES = 128
LOW_LANE = 64
COPIES = 112


def dense_kernel(
    depth, a0, a1, wg_hbm, wu_hbm, wd_hbm, out,
    x0, x1, wg, wu, wd, hid, acc, so, sr, b1, r1, b2, r2, b3, r3, wsem, ssem, rsem,
):
    rows = a0.shape[0]
    half = a1.shape[1]
    me = lax.axis_index("ep")
    side = lax.axis_index("side")
    plane = me // PLANE
    g0 = me % PLANE
    x, y = g0 % 2, g0 // 2
    gx = y * 2 + (1 - x)
    gy = (1 - y) * 2 + x
    gd = (1 - y) * 2 + (1 - x)
    base = plane * PLANE
    to_x, to_y = {"ep": base + gx}, {"ep": base + gy}
    to_side = {"side": 1 - side}
    def other(d):
        result, bit = plane, 1
        while bit < depth:
            if d & bit:
                result = result + bit - plane // bit % 2 * (2 * bit)
            bit *= 2
        return result

    to_plane = [None] + [{"ep": other(d) * PLANE + g0} for d in range(1, depth)]
    first, second = (to_x, to_y), (to_y, to_x)
    near, far = (gx, gy), (gy, gx)
    mesh_ids = pl.DeviceIdType.MESH
    started = []

    def send(src, dst, target):
        k = len(started)
        copy = pltpu.make_async_remote_copy(
            src_ref=src, dst_ref=dst, send_sem=ssem.at[k], recv_sem=rsem.at[k],
            device_id=target, device_id_type=mesh_ids,
        )
        copy.start()
        started.append(copy)
        return copy

    loads = [
        pltpu.make_async_copy(wg_hbm, wg, wsem.at[0]),
        pltpu.make_async_copy(wu_hbm, wu, wsem.at[1]),
        pltpu.make_async_copy(wd_hbm, wd, wsem.at[2]),
    ]
    for load in loads:
        load.start()

    barrier = pltpu.get_barrier_semaphore()
    partners = [to_x, to_y, to_side] + to_plane[1:]
    for target in partners:
        pl.semaphore_signal(barrier, inc=1, device_id=target, device_id_type=mesh_ids)
    pl.semaphore_wait(barrier, len(partners))

    own = (a0, a1)
    full = (x0, x1)
    order = list(range(depth - 1, -1, -1))

    def span(d):
        return pl.ds(pl.multiple_of(other(d) * rows, rows), rows)

    def slot(h, g, d):
        return full[h].at[g, side, span(d)]

    by_plane, by_first, by_second, by_far, by_side = {}, {}, {}, {}, {}

    def across(d):
        for h in range(2):
            by_plane[h, d] = send(own[h], slot(h, g0, 0), to_plane[d])

    def spread(d):
        for h in range(2):
            block = own[h] if d == 0 else slot(h, g0, d)
            by_first[h, d] = send(block, slot(h, g0, d), first[h])
        for h in range(2):
            block = own[h] if d == 0 else slot(h, g0, d)
            by_second[h, d] = send(block, slot(h, g0, d), second[h])
            by_side[h, 0, d] = send(block, slot(h, g0, d), to_side)

    def pass_on(d):
        for h in range(2):
            by_first[h, d].wait_recv()
            block = slot(h, near[h], d)
            by_far[h, d] = send(block, block, second[h])
            by_side[h, 1, d] = send(block, block, to_side)

    def collect(d):
        for h in range(2):
            by_second[h, d].wait_recv()
            block = slot(h, far[h], d)
            by_side[h, 2, d] = send(block, block, to_side)

    across(1)
    across(2)
    spread(0)
    for h in range(2):
        full[h][g0, side, span(0)] = own[h][...]
    pass_on(0)
    for d in range(1, depth):
        for h in range(2):
            by_plane[h, d].wait_recv()
        if 1 < d < depth - 1:
            across(d + 1)
        spread(d)
        pass_on(d)
        collect(d - 1)
    collect(depth - 1)

    lanes = lax.broadcasted_iota(jnp.int32, (1, GATE_LANES), 1)
    mine = (lanes == me) | (lanes == me + LOW_LANE)

    def both_sides(ref, g, columns):
        return jnp.concatenate([ref[g, side, :, columns], ref[g, 1 - side, :, columns]], axis=0)

    group_rows = x0.shape[2]
    wide = 256
    deep = 512

    def compute(g):
        tail = both_sides(x0, g, pl.ds(half, GATE_LANES)).astype(jnp.float32)
        share = jnp.sum(jnp.where(mine, tail, 0.0), axis=1, keepdims=True)

        @pl.loop(0, wg.shape[1] // wide)
        def _(n):
            columns = pl.ds(pl.multiple_of(n * wide, wide), wide)
            rows0 = both_sides(x0, g, pl.ds(0, half))
            rows1 = both_sides(x1, g, pl.ds(0, half))
            gate = jnp.dot(rows0, wg[pl.ds(0, half), columns], preferred_element_type=jnp.float32)
            gate += jnp.dot(rows1, wg[pl.ds(half, half), columns], preferred_element_type=jnp.float32)
            up = jnp.dot(rows0, wu[pl.ds(0, half), columns], preferred_element_type=jnp.float32)
            up += jnp.dot(rows1, wu[pl.ds(half, half), columns], preferred_element_type=jnp.float32)
            hidden = gate / (1.0 + jnp.exp(-gate)) * up * share
            hid[:, columns] = hidden.astype(jnp.bfloat16)

        @pl.loop(0, wd.shape[1] // deep)
        def _(n):
            columns = pl.ds(pl.multiple_of(n * deep, deep), deep)
            result = jnp.dot(hid[...], wd[:, columns], preferred_element_type=jnp.float32)
            acc[g, :, columns] = result[:group_rows]
            so[g, :, columns] = result[group_rows:].astype(jnp.bfloat16)

        return send(so.at[g], sr.at[g], to_side)

    def features(h):
        return pl.ds(h * half, half)

    def chip_sum(g, h, d):
        part = sr[g, span(d), features(h)].astype(jnp.float32)
        return acc[g, span(d), features(h)] + part

    def f32(ref, *index):
        return ref[index].astype(jnp.float32)

    back1, back2, back3 = {}, {}, {}

    def to_second(g, h, i, d):
        b1[h, i, d] = chip_sum(g, h, d).astype(jnp.bfloat16)
        back1[h, i, d] = send(b1.at[h, i, d], r1.at[h, i, d], second[h])

    def arrived(j, halves):
        for d in range(depth):
            for h in halves:
                by_side[h, j, d].wait_recv()

    for load in loads:
        load.wait()
    arrived(0, (0, 1))
    side0 = compute(g0)
    arrived(1, (0,))
    arrived(2, (1,))
    sidex = compute(gx)
    arrived(1, (1,))
    arrived(2, (0,))
    for d in range(depth):
        for h in range(2):
            by_far[h, d].wait_recv()
            block = slot(h, gd, d)
            by_side[h, 3, d] = send(block, block, to_side)
    sidex.wait_recv()
    for d in order:
        to_second(gx, 1, 0, d)
    sidey = compute(gy)
    arrived(3, (0, 1))
    sidey.wait_recv()
    for d in order:
        to_second(gy, 0, 0, d)
    sided = compute(gd)
    side0.wait_recv()
    sided.wait_recv()
    def diagonal(i):
        for h in range(2):
            to_second(gd, h, 1, order[i])

    for i in range(2):
        diagonal(i)

    def to_first(h, d):
        back1[h, 1, d].wait_recv()
        total = chip_sum(near[h], h, d) + f32(r1, h, 1, d)
        b2[h, d] = total.astype(jnp.bfloat16)
        back2[h, d] = send(b2.at[h, d], r2.at[h, d], first[h])

    def plane_sum(h, d):
        back1[h, 0, d].wait_recv()
        back2[h, d].wait_recv()
        return chip_sum(g0, h, d) + f32(r1, h, 0, d) + f32(r2, h, d)

    def to_owner(h, d):
        b3[h, d - 1] = plane_sum(h, d).astype(jnp.bfloat16)
        back3[h, d] = send(b3.at[h, d - 1], r3.at[h, d - 1], to_plane[d])

    for i, d in enumerate(order):
        for h in range(2):
            to_first(h, d)
        if i + 2 < depth:
            diagonal(i + 2)
        if i > 0:
            for h in range(2):
                to_owner(h, order[i - 1])
    for h in range(2):
        total = plane_sum(h, 0)
        for d in range(1, depth):
            back3[h, d].wait_recv()
            total += f32(r3, h, d - 1)
        out[:, features(h)] = total.astype(jnp.bfloat16)
    for copy in started:
        copy.wait_send()


def dense_moe(normed, dense, gate_matrix, up_matrix, down_matrix):
    count, width = normed.shape
    devices, experts = lax.axis_size("ep"), dense.shape[1]
    half = width // 2
    depth = devices // PLANE
    high = dense.astype(jnp.bfloat16)
    low = (dense - high.astype(jnp.float32)).astype(jnp.bfloat16)
    pad = jnp.zeros((count, LOW_LANE - experts), jnp.bfloat16)
    a0 = jnp.concatenate([normed[:, :half], high, pad, low, pad], axis=1)
    a1 = normed[:, half:]
    rows = depth * count
    bf16 = jnp.bfloat16
    vmem = pl.BlockSpec(memory_space=pltpu.VMEM)
    hbm = pl.BlockSpec(memory_space=pl.ANY)
    hidden_units = gate_matrix.shape[1]
    return pl.pallas_call(
        functools.partial(dense_kernel, depth),
        out_shape=jax.ShapeDtypeStruct((count, width), bf16),
        in_specs=[vmem, vmem, hbm, hbm, hbm],
        out_specs=vmem,
        scratch_shapes=[
            pltpu.VMEM((PLANE, 2, rows, half + GATE_LANES), bf16),
            pltpu.VMEM((PLANE, 2, rows, half), bf16),
            pltpu.VMEM(gate_matrix.shape, bf16),
            pltpu.VMEM(up_matrix.shape, bf16),
            pltpu.VMEM(down_matrix.shape, bf16),
            pltpu.VMEM((2 * rows, hidden_units), bf16),
            pltpu.VMEM((PLANE, rows, width), jnp.float32),
            pltpu.VMEM((PLANE, rows, width), bf16),
            pltpu.VMEM((PLANE, rows, width), bf16),
            pltpu.VMEM((2, 2, depth, count, half), bf16),
            pltpu.VMEM((2, 2, depth, count, half), bf16),
            pltpu.VMEM((2, depth, count, half), bf16),
            pltpu.VMEM((2, depth, count, half), bf16),
            pltpu.VMEM((2, depth - 1, count, half), bf16),
            pltpu.VMEM((2, depth - 1, count, half), bf16),
            pltpu.SemaphoreType.DMA((3,)),
            pltpu.SemaphoreType.DMA((COPIES,)),
            pltpu.SemaphoreType.DMA((COPIES,)),
        ],
        compiler_params=pltpu.CompilerParams(
            collective_id=0, has_side_effects=True, vmem_limit_bytes=56 * 1024 * 1024
        ),
        cost_estimate=pl.CostEstimate(
            flops=12 * PLANE * rows * width * hidden_units,
            bytes_accessed=6 * width * hidden_units,
            transcendentals=0,
        ),
    )(a0, a1, gate_matrix, up_matrix, down_matrix)


def body(queries, latents, lengths, tokens, routes, router, gate_weight, up_weight, down_weight):
    attended = jax.vmap(attend_request)(queries, latents, lengths)
    experts = lax.axis_size("ep")
    token_count, top_count = routes.shape
    width = tokens.shape[1]
    capacity = min(token_count, 2 * token_count * top_count // experts)
    values = tokens.astype(jnp.float32)
    mean_square = jnp.mean(values * values, axis=1, keepdims=True)
    normed = (values * lax.rsqrt(mean_square + NORM_EPS)).astype(jnp.bfloat16)
    affinity = jax.nn.sigmoid(jnp.dot(normed, router, preferred_element_type=jnp.float32))
    one_hot = routes[:, :, None] == lax.broadcasted_iota(jnp.int32, (1, 1, experts), 2)
    chosen = jnp.sum(jnp.where(one_hot, affinity[:, None, :], 0.0), axis=2)
    gates = chosen / jnp.sum(chosen, axis=1, keepdims=True) * ROUTE_SCALE
    if capacity == token_count and experts in (8, 16, 32, 64) and experts <= LOW_LANE:
        dense = jnp.sum(jnp.where(one_hot, gates[:, :, None], 0.0), axis=1)
        moe = dense_moe(normed, dense, gate_weight[0], up_weight[0], down_weight[0])
        return (attended, moe)
    flat_hot = one_hot.reshape(-1, experts).astype(jnp.int32)
    slot = jnp.sum((jnp.cumsum(flat_hot, axis=0) - flat_hot) * flat_hot, axis=1)
    counts = jnp.sum(flat_hot, axis=0)
    target = routes.reshape(-1) * capacity + slot
    outgoing = (
        jnp.zeros((experts * capacity, width), jnp.bfloat16)
        .at[target]
        .set(jnp.repeat(normed, top_count, axis=0))
    )
    outgoing = outgoing.reshape(experts, capacity, width)
    gate_matrix = gate_weight[0]
    up_matrix = up_weight[0]
    down_matrix = down_weight[0]
    arrived, arrived_counts = (
        lax.all_to_all(outgoing, "ep", split_axis=0, concat_axis=0, tiled=True),
        lax.all_to_all(counts, "ep", split_axis=0, concat_axis=0, tiled=True),
    )
    paired, paired_counts = (
        lax.all_gather(arrived, "side", axis=0, tiled=True),
        lax.all_gather(arrived_counts, "side", axis=0, tiled=True),
    )
    paired_rows = paired.reshape(-1, width)
    valid = slot_mask(paired_counts, capacity)
    summed = lax.psum_scatter(
        expert_rows(paired_rows, valid, gate_matrix, up_matrix, down_matrix),
        "side",
        scatter_dimension=0,
        tiled=True,
    )
    returned = lax.all_to_all(
        summed.astype(jnp.bfloat16).reshape(experts, capacity, width),
        "ep",
        split_axis=0,
        concat_axis=0,
        tiled=True,
    )
    picked = returned.reshape(experts * capacity, width)[target]
    weighted = picked.reshape(token_count, top_count, width).astype(jnp.float32) * gates[:, :, None]
    moe = jnp.sum(weighted, axis=1)
    return (attended, moe.astype(jnp.bfloat16))


def solution(mesh):
    return jax.shard_map(
        body,
        mesh=mesh,
        in_specs=(
            P(("groups", "ep", "side"), None),
            P(("groups", "ep", "side"), None, None),
            P(("groups", "ep", "side")),
            P(("groups", "ep", "side"), None),
            P(("groups", "ep", "side"), None),
            P(),
            P("ep", None, "side"),
            P("ep", None, "side"),
            P("ep", "side", None),
        ),
        out_specs=(P(("groups", "ep", "side"), None), P(("groups", "ep", "side"), None)),
        check_vma=False,
    )
```

```python
import functools

import jax
import jax.numpy as jnp
from jax import lax
from jax.experimental import pallas as pl
from jax.experimental.pallas import tpu as pltpu
from jax.sharding import PartitionSpec as P

LATENT = 512


SOFT_SCALE = 192.0 ** (-0.5)
ROUTE_SCALE = 2.5
NORM_EPS = 1e-06


def attend_request(query_row, cache_block, length):
    positions = cache_block.shape[1]
    head_queries = query_row.reshape(-1, cache_block.shape[0])
    scores = jnp.dot(head_queries, cache_block, preferred_element_type=jnp.float32) * SOFT_SCALE
    live = lax.broadcasted_iota(jnp.int32, (1, positions), 1) < length
    scores = jnp.where(live, scores, -1e30)
    highest = jnp.max(scores, axis=1, keepdims=True)
    powers = jnp.where(live, jnp.exp(scores - highest), 0.0)
    probs = (powers / jnp.sum(powers, axis=1, keepdims=True)).astype(jnp.bfloat16)
    mixed = lax.dot_general(
        probs, cache_block[:LATENT], (((1,), (1,)), ((), ())), preferred_element_type=jnp.float32
    )
    return mixed.astype(jnp.bfloat16).reshape(-1)


def expert_block(rows, gate_matrix, up_matrix, down_matrix):
    gate = jnp.dot(rows, gate_matrix, preferred_element_type=jnp.float32)
    up = jnp.dot(rows, up_matrix, preferred_element_type=jnp.float32)
    hidden = (jax.nn.silu(gate) * up).astype(jnp.bfloat16)
    return jnp.dot(hidden, down_matrix, preferred_element_type=jnp.float32)


def expert_rows(rows, valid, gate_matrix, up_matrix, down_matrix):
    return jnp.where(valid[:, None], expert_block(rows, gate_matrix, up_matrix, down_matrix), 0.0)


def slot_mask(counts, capacity):
    return (
        lax.broadcasted_iota(jnp.int32, (counts.shape[0], capacity), 1) < counts[:, None]
    ).reshape(-1)


PLANE = 4
GATE_LANES = 128
LOW_LANE = 64
COPIES = 112


def dense_kernel(
    depth, a0, a1, wg_hbm, wu_hbm, wd_hbm, out,
    x0, x1, wg, wu, wd, hid, acc, so, sr, b1, r1, b2, r2, b3, r3, wsem, ssem, rsem,
):
    rows = a0.shape[0]
    half = a1.shape[1]
    me = lax.axis_index("ep")
    side = lax.axis_index("side")
    plane = me // PLANE
    g0 = me % PLANE
    x, y = g0 % 2, g0 // 2
    gx = y * 2 + (1 - x)
    gy = (1 - y) * 2 + x
    gd = (1 - y) * 2 + (1 - x)
    base = plane * PLANE
    to_x, to_y = {"ep": base + gx}, {"ep": base + gy}
    to_side = {"side": 1 - side}
    def other(d):
        result, bit = plane, 1
        while bit < depth:
            if d & bit:
                result = result + bit - plane // bit % 2 * (2 * bit)
            bit *= 2
        return result

    to_plane = [None] + [{"ep": other(d) * PLANE + g0} for d in range(1, depth)]
    first, second = (to_x, to_y), (to_y, to_x)
    near, far = (gx, gy), (gy, gx)
    mesh_ids = pl.DeviceIdType.MESH
    started = []

    def send(src, dst, target):
        k = len(started)
        copy = pltpu.make_async_remote_copy(
            src_ref=src, dst_ref=dst, send_sem=ssem.at[k], recv_sem=rsem.at[k],
            device_id=target, device_id_type=mesh_ids,
        )
        copy.start()
        started.append(copy)
        return copy

    loads = [
        pltpu.make_async_copy(wg_hbm, wg, wsem.at[0]),
        pltpu.make_async_copy(wu_hbm, wu, wsem.at[1]),
        pltpu.make_async_copy(wd_hbm, wd, wsem.at[2]),
    ]
    for load in loads:
        load.start()

    barrier = pltpu.get_barrier_semaphore()
    partners = [to_x, to_y, to_side] + to_plane[1:]
    for target in partners:
        pl.semaphore_signal(barrier, inc=1, device_id=target, device_id_type=mesh_ids)
    pl.semaphore_wait(barrier, len(partners))

    own = (a0, a1)
    full = (x0, x1)
    order = list(range(depth - 1, -1, -1))

    def span(d):
        return pl.ds(pl.multiple_of(other(d) * rows, rows), rows)

    def slot(h, g, d):
        return full[h].at[g, side, span(d)]

    by_plane, by_first, by_second, by_far, by_side = {}, {}, {}, {}, {}

    def across(d):
        for h in range(2):
            by_plane[h, d] = send(own[h], slot(h, g0, 0), to_plane[d])

    def spread(d):
        for h in range(2):
            block = own[h] if d == 0 else slot(h, g0, d)
            by_first[h, d] = send(block, slot(h, g0, d), first[h])
        for h in range(2):
            block = own[h] if d == 0 else slot(h, g0, d)
            by_second[h, d] = send(block, slot(h, g0, d), second[h])
            by_side[h, 0, d] = send(block, slot(h, g0, d), to_side)

    def pass_on(d):
        for h in range(2):
            by_first[h, d].wait_recv()
            block = slot(h, near[h], d)
            by_far[h, d] = send(block, block, second[h])
            by_side[h, 1, d] = send(block, block, to_side)

    def collect(d):
        for h in range(2):
            by_second[h, d].wait_recv()
            block = slot(h, far[h], d)
            by_side[h, 2, d] = send(block, block, to_side)

    across(1)
    across(2)
    spread(0)
    for h in range(2):
        full[h][g0, side, span(0)] = own[h][...]
    pass_on(0)
    for d in range(1, depth):
        for h in range(2):
            by_plane[h, d].wait_recv()
        if 1 < d < depth - 1:
            across(d + 1)
        spread(d)
        pass_on(d)
        collect(d - 1)
    collect(depth - 1)

    lanes = lax.broadcasted_iota(jnp.int32, (1, GATE_LANES), 1)
    mine = (lanes == me) | (lanes == me + LOW_LANE)

    def both_sides(ref, g, columns):
        return jnp.concatenate([ref[g, side, :, columns], ref[g, 1 - side, :, columns]], axis=0)

    group_rows = x0.shape[2]
    wide = 256
    deep = 512

    def compute(g):
        tail = both_sides(x0, g, pl.ds(half, GATE_LANES)).astype(jnp.float32)
        share = jnp.sum(jnp.where(mine, tail, 0.0), axis=1, keepdims=True)

        @pl.loop(0, wg.shape[1] // wide)
        def _(n):
            columns = pl.ds(pl.multiple_of(n * wide, wide), wide)
            rows0 = both_sides(x0, g, pl.ds(0, half))
            rows1 = both_sides(x1, g, pl.ds(0, half))
            gate = jnp.dot(rows0, wg[pl.ds(0, half), columns], preferred_element_type=jnp.float32)
            gate += jnp.dot(rows1, wg[pl.ds(half, half), columns], preferred_element_type=jnp.float32)
            up = jnp.dot(rows0, wu[pl.ds(0, half), columns], preferred_element_type=jnp.float32)
            up += jnp.dot(rows1, wu[pl.ds(half, half), columns], preferred_element_type=jnp.float32)
            hidden = gate / (1.0 + jnp.exp(-gate)) * up * share
            hid[:, columns] = hidden.astype(jnp.bfloat16)

        @pl.loop(0, wd.shape[1] // deep)
        def _(n):
            columns = pl.ds(pl.multiple_of(n * deep, deep), deep)
            result = jnp.dot(hid[...], wd[:, columns], preferred_element_type=jnp.float32)
            acc[g, :, columns] = result[:group_rows]
            so[g, :, columns] = result[group_rows:].astype(jnp.bfloat16)

        return send(so.at[g], sr.at[g], to_side)

    def features(h):
        return pl.ds(h * half, half)

    def chip_sum(g, h, d):
        part = sr[g, span(d), features(h)].astype(jnp.float32)
        return acc[g, span(d), features(h)] + part

    def f32(ref, *index):
        return ref[index].astype(jnp.float32)

    back1, back2, back3 = {}, {}, {}

    def to_second(g, h, i, d):
        b1[h, i, d] = chip_sum(g, h, d).astype(jnp.bfloat16)
        back1[h, i, d] = send(b1.at[h, i, d], r1.at[h, i, d], second[h])

    def arrived(j, halves):
        for d in range(depth):
            for h in halves:
                by_side[h, j, d].wait_recv()

    for load in loads:
        load.wait()
    arrived(0, (0, 1))
    side0 = compute(g0)
    arrived(1, (0,))
    arrived(2, (1,))
    sidex = compute(gx)
    arrived(1, (1,))
    arrived(2, (0,))
    sidex.wait_recv()
    for d in order:
        to_second(gx, 1, 0, d)
    sidey = compute(gy)
    for d in range(depth):
        for h in range(2):
            by_far[h, d].wait_recv()
            block = slot(h, gd, d)
            by_side[h, 3, d] = send(block, block, to_side)
    arrived(3, (0, 1))
    sidey.wait_recv()
    for d in order:
        to_second(gy, 0, 0, d)
    sided = compute(gd)
    side0.wait_recv()
    sided.wait_recv()
    def diagonal(i):
        for h in range(2):
            to_second(gd, h, 1, order[i])

    for i in range(2):
        diagonal(i)

    def to_first(h, d):
        back1[h, 1, d].wait_recv()
        total = chip_sum(near[h], h, d) + f32(r1, h, 1, d)
        b2[h, d] = total.astype(jnp.bfloat16)
        back2[h, d] = send(b2.at[h, d], r2.at[h, d], first[h])

    def plane_sum(h, d):
        back1[h, 0, d].wait_recv()
        back2[h, d].wait_recv()
        return chip_sum(g0, h, d) + f32(r1, h, 0, d) + f32(r2, h, d)

    def to_owner(h, d):
        b3[h, d - 1] = plane_sum(h, d).astype(jnp.bfloat16)
        back3[h, d] = send(b3.at[h, d - 1], r3.at[h, d - 1], to_plane[d])

    for i, d in enumerate(order):
        for h in range(2):
            to_first(h, d)
        if i + 2 < depth:
            diagonal(i + 2)
        if i > 0:
            for h in range(2):
                to_owner(h, order[i - 1])
    for h in range(2):
        total = plane_sum(h, 0)
        for d in range(1, depth):
            back3[h, d].wait_recv()
            total += f32(r3, h, d - 1)
        out[:, features(h)] = total.astype(jnp.bfloat16)
    for copy in started:
        copy.wait_send()


def dense_moe(normed, dense, gate_matrix, up_matrix, down_matrix):
    count, width = normed.shape
    devices, experts = lax.axis_size("ep"), dense.shape[1]
    half = width // 2
    depth = devices // PLANE
    high = dense.astype(jnp.bfloat16)
    low = (dense - high.astype(jnp.float32)).astype(jnp.bfloat16)
    pad = jnp.zeros((count, LOW_LANE - experts), jnp.bfloat16)
    a0 = jnp.concatenate([normed[:, :half], high, pad, low, pad], axis=1)
    a1 = normed[:, half:]
    rows = depth * count
    bf16 = jnp.bfloat16
    vmem = pl.BlockSpec(memory_space=pltpu.VMEM)
    hbm = pl.BlockSpec(memory_space=pl.ANY)
    hidden_units = gate_matrix.shape[1]
    return pl.pallas_call(
        functools.partial(dense_kernel, depth),
        out_shape=jax.ShapeDtypeStruct((count, width), bf16),
        in_specs=[vmem, vmem, hbm, hbm, hbm],
        out_specs=vmem,
        scratch_shapes=[
            pltpu.VMEM((PLANE, 2, rows, half + GATE_LANES), bf16),
            pltpu.VMEM((PLANE, 2, rows, half), bf16),
            pltpu.VMEM(gate_matrix.shape, bf16),
            pltpu.VMEM(up_matrix.shape, bf16),
            pltpu.VMEM(down_matrix.shape, bf16),
            pltpu.VMEM((2 * rows, hidden_units), bf16),
            pltpu.VMEM((PLANE, rows, width), jnp.float32),
            pltpu.VMEM((PLANE, rows, width), bf16),
            pltpu.VMEM((PLANE, rows, width), bf16),
            pltpu.VMEM((2, 2, depth, count, half), bf16),
            pltpu.VMEM((2, 2, depth, count, half), bf16),
            pltpu.VMEM((2, depth, count, half), bf16),
            pltpu.VMEM((2, depth, count, half), bf16),
            pltpu.VMEM((2, depth - 1, count, half), bf16),
            pltpu.VMEM((2, depth - 1, count, half), bf16),
            pltpu.SemaphoreType.DMA((3,)),
            pltpu.SemaphoreType.DMA((COPIES,)),
            pltpu.SemaphoreType.DMA((COPIES,)),
        ],
        compiler_params=pltpu.CompilerParams(
            collective_id=0, has_side_effects=True, vmem_limit_bytes=56 * 1024 * 1024
        ),
        cost_estimate=pl.CostEstimate(
            flops=12 * PLANE * rows * width * hidden_units,
            bytes_accessed=6 * width * hidden_units,
            transcendentals=0,
        ),
    )(a0, a1, gate_matrix, up_matrix, down_matrix)


def body(queries, latents, lengths, tokens, routes, router, gate_weight, up_weight, down_weight):
    attended = jax.vmap(attend_request)(queries, latents, lengths)
    experts = lax.axis_size("ep")
    token_count, top_count = routes.shape
    width = tokens.shape[1]
    capacity = min(token_count, 2 * token_count * top_count // experts)
    values = tokens.astype(jnp.float32)
    mean_square = jnp.mean(values * values, axis=1, keepdims=True)
    normed = (values * lax.rsqrt(mean_square + NORM_EPS)).astype(jnp.bfloat16)
    affinity = jax.nn.sigmoid(jnp.dot(normed, router, preferred_element_type=jnp.float32))
    one_hot = routes[:, :, None] == lax.broadcasted_iota(jnp.int32, (1, 1, experts), 2)
    chosen = jnp.sum(jnp.where(one_hot, affinity[:, None, :], 0.0), axis=2)
    gates = chosen / jnp.sum(chosen, axis=1, keepdims=True) * ROUTE_SCALE
    if capacity == token_count and experts in (8, 16, 32, 64) and experts <= LOW_LANE:
        dense = jnp.sum(jnp.where(one_hot, gates[:, :, None], 0.0), axis=1)
        moe = dense_moe(normed, dense, gate_weight[0], up_weight[0], down_weight[0])
        return (attended, moe)
    flat_hot = one_hot.reshape(-1, experts).astype(jnp.int32)
    slot = jnp.sum((jnp.cumsum(flat_hot, axis=0) - flat_hot) * flat_hot, axis=1)
    counts = jnp.sum(flat_hot, axis=0)
    target = routes.reshape(-1) * capacity + slot
    outgoing = (
        jnp.zeros((experts * capacity, width), jnp.bfloat16)
        .at[target]
        .set(jnp.repeat(normed, top_count, axis=0))
    )
    outgoing = outgoing.reshape(experts, capacity, width)
    gate_matrix = gate_weight[0]
    up_matrix = up_weight[0]
    down_matrix = down_weight[0]
    arrived, arrived_counts = (
        lax.all_to_all(outgoing, "ep", split_axis=0, concat_axis=0, tiled=True),
        lax.all_to_all(counts, "ep", split_axis=0, concat_axis=0, tiled=True),
    )
    paired, paired_counts = (
        lax.all_gather(arrived, "side", axis=0, tiled=True),
        lax.all_gather(arrived_counts, "side", axis=0, tiled=True),
    )
    paired_rows = paired.reshape(-1, width)
    valid = slot_mask(paired_counts, capacity)
    summed = lax.psum_scatter(
        expert_rows(paired_rows, valid, gate_matrix, up_matrix, down_matrix),
        "side",
        scatter_dimension=0,
        tiled=True,
    )
    returned = lax.all_to_all(
        summed.astype(jnp.bfloat16).reshape(experts, capacity, width),
        "ep",
        split_axis=0,
        concat_axis=0,
        tiled=True,
    )
    picked = returned.reshape(experts * capacity, width)[target]
    weighted = picked.reshape(token_count, top_count, width).astype(jnp.float32) * gates[:, :, None]
    moe = jnp.sum(weighted, axis=1)
    return (attended, moe.astype(jnp.bfloat16))


def solution(mesh):
    return jax.shard_map(
        body,
        mesh=mesh,
        in_specs=(
            P(("groups", "ep", "side"), None),
            P(("groups", "ep", "side"), None, None),
            P(("groups", "ep", "side")),
            P(("groups", "ep", "side"), None),
            P(("groups", "ep", "side"), None),
            P(),
            P("ep", None, "side"),
            P("ep", None, "side"),
            P("ep", "side", None),
        ),
        out_specs=(P(("groups", "ep", "side"), None), P(("groups", "ep", "side"), None)),
        check_vma=False,
    )
```
